512 devices in a mesh: sub: 128 (over x, z_lo, y, core), mode: 4 (over z_hi).
Axes of the slice: x: 4, y: 8, z: 8 (z_hi: 4, z_lo: 2; z = z_hi * 2 + z_lo), core: 2. Of those that a mesh axis runs over, the one named last changes fastest.
Arguments:
- leaf_coords: bfloat16 [1024, 768, 128], P('sub', 'mode'), may hold values from -6 to 6
- leaf_modes: bfloat16 [1024, 128, 512], P('sub'), may hold values from -0.5 to 0.5
- constraint_modes: bfloat16 [1024, 3, 256, 512], P('sub'), may hold values from -0.375 to 0.375
- sep_one: bfloat16 [768, 16384], P('mode', 'sub'), may hold values from -6 to 6
- sep_two: bfloat16 [768, 8192], P('mode', 'sub'), may hold values from -6 to 6
- sep_three: bfloat16 [768, 4096], P('mode', 'sub'), may hold values from -6 to 6
- cluster_rows: int32 [384, 512], P('sub'), may hold values from 0 to 524287, as said below
- operators: bfloat16 [384, 512, 384], P('sub'), may hold values from -0.25 to 0.25
- compliance: float32 [384, 384], P('sub'), may hold values from 0.05 to 0.5
- modal_weight: float32 [768], P('mode'), may hold values from 0.5 to 2
Outputs:
- stresses: float32 [384, 768, 384], P('sub', 'mode')
- strain_energy: float32 [24576], P(('sub', 'mode'))
The draws below stay inside these ranges and needn't reach their ends.
Inputs may be any that keep to these rules, and one draw needn't show every extreme that they name: cluster_rows[c, j] = s * 4096 + r names column r of the displacement columns of the leaves of sub index s (its leaves laid end to end). The clusters of sub index d read only from sub indices d - 2 to d + 2 taken around the axis, and at most 384 of their 1536 rows from any one of these indices; that most is reached for every d from one of the five.
All inputs are finite; a program needn't handle non-finite values.
Results may differ from the reference program's by a relative error of at most 0.0029.
Values may be sent and summed in bfloat16 or wider, within the bound.
A program may use at most 64 MiB of HBM per device.

```python
import math
import jax
import jax.numpy as jnp
from jax import lax

M = 768
B = 256
R = 512
KL = 128
CW = 512
PTS = 64
LEAF_DEV = 8
CL_DEV = 3
SR = 384
LEAVES = 1024
CLUSTERS = 384
DOFS = 4096
SEP_ONE = 16384
SEP_TWO = 8192
SEP_THREE = 4096


def draw_cluster_rows(key, part):
    key = jax.random.fold_in(key, 11)
    devices = CLUSTERS // CL_DEV
    slots = CL_DEV * CW
    first, second, third, fourth = jax.random.split(key, 4)
    swing = jax.random.randint(first, (devices, 2), -(slots // 16), slots // 16 + 1)
    middle = slots // 8 + slots // 16
    others = middle + jnp.stack([swing[:, 0], -swing[:, 0], swing[:, 1], -swing[:, 1]], axis=1)
    counts = jnp.concatenate([jnp.full((devices, 1), slots // 4, jnp.int32), others.astype(jnp.int32)], axis=1)
    scores = jax.random.randint(second, (devices, 5), 0, 1000) * 8 + jnp.arange(5, dtype=jnp.int32)[None, :]
    group_offset = jnp.argsort(scores, axis=1).astype(jnp.int32) - 2
    bounds = jnp.cumsum(counts, axis=1)
    position = jnp.arange(slots, dtype=jnp.int32)
    group = jnp.sum((position[None, :, None] >= bounds[:, None, :]).astype(jnp.int32), axis=2)
    slot_offset = jnp.take_along_axis(group_offset, group, axis=1)
    shuffle_keys = jax.random.randint(third, (devices, slots), 0, 1 << 14) * slots + position[None, :]
    shuffle = jnp.argsort(shuffle_keys, axis=1)
    slot_offset = jnp.take_along_axis(slot_offset, shuffle, axis=1)
    device_ids = jnp.arange(devices, dtype=jnp.int32)[:, None]
    source = (device_ids + slot_offset) % devices
    row_in = jax.random.randint(fourth, (devices, slots), 0, DOFS)
    flat = source * DOFS + row_in
    return flat.reshape(CLUSTERS, CW).astype(jnp.int32)


def level_of(key, shape, cuts, low, top_value):
    level, own = 1.0, jax.random.fold_in(key, 6)
    for dim, blocks in cuts:
        heights = jnp.exp(jax.random.uniform(jax.random.fold_in(own, dim), (blocks,), jnp.float32, low / len(cuts), top_value / len(cuts)))
        level = level * jnp.repeat(heights, shape[dim] // blocks).reshape([-1 if axis == dim else 1 for axis in range(len(shape))])
    return level


def noise(stream_key, shape, deviation, reach, cuts=(), held_as=jnp.bfloat16):
    result = deviation * jax.random.normal(stream_key, shape, jnp.float32)
    if cuts:
        result = result * level_of(stream_key, shape, cuts, -0.22, 0.18)
    return jnp.clip(result, -reach, reach).astype(held_as)


def setup_inputs(seed: int = 0) -> dict:
    keys = jax.random.split(jax.random.key(seed), 11)
    leaf_coords = noise(keys[0], (LEAVES, M, KL), 1.0, 6.0, ((0, 128), (1, 4)))
    leaf_modes = noise(keys[1], (LEAVES, KL, R), KL ** -0.5, 0.5, ((0, 128),))
    constraint_modes = noise(keys[2], (LEAVES, 3, B, R), B ** -0.5, 0.375, ((0, 128),))
    sep_one = noise(keys[3], (M, SEP_ONE), 1.0, 6.0, ((0, 4), (1, 128)))
    sep_two = noise(keys[4], (M, SEP_TWO), 1.0, 6.0, ((0, 4), (1, 128)))
    sep_three = noise(keys[5], (M, SEP_THREE), 1.0, 6.0, ((0, 4), (1, 128)))
    cluster_rows = draw_cluster_rows(jax.random.fold_in(keys[10], 71), 0)
    operators = noise(keys[7], (CLUSTERS, CW, SR), CW ** -0.5, 0.25, ((0, 128),))
    compliance = jnp.clip(jnp.exp(math.log(0.5) - 2.3025851 * jax.random.uniform(keys[8], (CLUSTERS, SR), jnp.float32) ** level_of(keys[8], (CLUSTERS, SR), ((0, 128),), -0.2, 0.2)), 0.05, 0.5)
    modal_weight = jnp.clip(jnp.exp(math.log(2.0) - 1.3862944 * jax.random.uniform(keys[9], (M,), jnp.float32) ** level_of(keys[9], (M,), ((0, 4),), -0.2, 0.2)), 0.5, 2.0)
    return dict(leaf_coords=leaf_coords, leaf_modes=leaf_modes, constraint_modes=constraint_modes, sep_one=sep_one, sep_two=sep_two, sep_three=sep_three, cluster_rows=cluster_rows, operators=operators, compliance=compliance, modal_weight=modal_weight)


def reference(leaf_coords, leaf_modes, constraint_modes, sep_one, sep_two, sep_three, cluster_rows, operators, compliance, modal_weight):
    separators = (sep_one, sep_two, sep_three)

    def one_leaf(leaf):
        device = leaf // LEAF_DEV
        total = jnp.dot(leaf_coords[leaf].astype(jnp.float32), leaf_modes[leaf].astype(jnp.float32), preferred_element_type=jnp.float32)
        for level in range(3):
            node = (device >> (level + 1)).astype(jnp.int32)
            block = lax.dynamic_slice(separators[level], (jnp.int32(0), (node * B).astype(jnp.int32)), (M, B))
            total = total + jnp.dot(block.astype(jnp.float32), constraint_modes[leaf, level].astype(jnp.float32), preferred_element_type=jnp.float32)
        return total.astype(jnp.bfloat16)

    displaced = lax.map(one_leaf, jnp.arange(LEAVES, dtype=jnp.int32))
    flat = jnp.transpose(displaced, (1, 0, 2)).reshape(M, LEAVES * R)

    def one_cluster(inputs):
        row_ids, operator, weights = inputs
        gathered = jnp.take(flat, row_ids, axis=1)
        stress = jnp.dot(gathered.astype(jnp.float32), operator.astype(jnp.float32), preferred_element_type=jnp.float32)
        weighted = jnp.sum(modal_weight[:, None] * stress * stress, axis=0) * weights
        energy = jnp.sum(weighted.reshape(6, PTS), axis=0) * (0.5 / M)
        return stress, energy

    stresses, energies = lax.map(one_cluster, (cluster_rows, operators, compliance))
    return stresses, energies.reshape(CLUSTERS * PTS)
```

```python
import functools

import jax
import jax.numpy as jnp
from jax import lax
from jax.experimental import pallas as pl
from jax.experimental.pallas import tpu as pltpu
from jax.sharding import PartitionSpec as P

M = 768
F32, BF16 = jnp.float32, jnp.bfloat16
MODES, NLEAF, KL, R, B = 192, 8, 128, 512, 256
DOFS = NLEAF * R
CLS, CW, SR = 3, 512, 384
SLOT, NOFF = 384, 5
MESH = pl.DeviceIdType.MESH


def mm(a, b):
    return jnp.dot(a, b, preferred_element_type=F32)


def one_hot(table, values):
    n, w = table.shape[0], values.shape[1]
    wide = jnp.broadcast_to(values, (16, w)).astype(BF16).reshape(1, 16, w)
    rows = jnp.concatenate([table.reshape(n // 16, 16, 128)] * (w // 128), axis=2)
    hit = rows == jnp.broadcast_to(wide, (n // 16, 16, w))
    return jnp.where(hit, jnp.ones((), BF16), jnp.zeros((), BF16)).reshape(n, w)


def kernel(
    subs,
    peers_mode,
    lc_h,
    lm_h,
    cm_h,
    s1_h,
    s2_h,
    s3_h,
    rows_h,
    ops_h,
    comp_h,
    mw_h,
    stress,
    energy,
    lc,
    w,
    a1,
    a2,
    a3,
    x23,
    rows,
    ops,
    comp,
    mw,
    acc,
    disp,
    table,
    pick,
    perm,
    lists,
    want,
    hot,
    gath,
    got,
    sacc,
    terms,
    in_sem,
    leaf_sem,
    cm_sem,
    sep_send,
    sep_recv,
    list_send,
    list_recv,
    data_send,
    data_recv,
    en_send,
    en_recv,
):
    me = lax.axis_index("sub")
    mo = lax.axis_index("mode")
    odd = lax.rem(me, 2)
    in_eight = lax.rem(me, 8)
    in_four = lax.rem(me, 4)
    rows[...] = jnp.full(rows.shape, -1, jnp.int32)

    own1 = a1.at[:, pl.ds(pl.multiple_of(odd * 128, 128), 128)]
    own2 = a2.at[pl.ds(pl.multiple_of(in_four * 64, 64), 64), :]
    own3 = a3.at[pl.ds(pl.multiple_of(in_eight * 32, 32), 32), :]
    loads = [
        pltpu.make_async_copy(s3_h, own3, in_sem.at[0]),
        pltpu.make_async_copy(s2_h, own2, in_sem.at[1]),
        pltpu.make_async_copy(s1_h, own1, in_sem.at[2]),
        pltpu.make_async_copy(rows_h, rows.at[pl.ds(0, CLS), :], in_sem.at[3]),
        pltpu.make_async_copy(lc_h, lc, in_sem.at[4]),
        pltpu.make_async_copy(comp_h, comp, in_sem.at[5]),
        pltpu.make_async_copy(mw_h, mw, in_sem.at[6]),
        pltpu.make_async_copy(ops_h, ops, in_sem.at[7]),
    ]
    for load in loads[:7]:
        load.start()

    def leaf_load(l):
        return pltpu.make_async_copy(lm_h.at[l], w.at[l, pl.ds(0, KL), :], leaf_sem.at[l])

    def cm_load(l):
        return pltpu.make_async_copy(cm_h.at[l], w.at[l, pl.ds(KL, 3 * B), :], cm_sem.at[l])

    @pl.loop(0, NLEAF)
    def _(l):
        leaf_load(l).start()
        cm_load(l).start()

    loads[7].start()

    def at_sub(offset):
        return lax.rem(me + offset + subs, subs)

    def in_group(x):
        return me - in_eight + jnp.bitwise_xor(in_eight, x)

    barrier = pltpu.get_barrier_semaphore()
    greeted = 0
    for x in range(1, 8):
        pl.semaphore_signal(barrier, inc=1, device_id=(in_group(x), mo), device_id_type=MESH)
        greeted += 1
    for q in (-2, -1, 1, 2):
        pl.semaphore_signal(barrier, inc=1, device_id=(at_sub(q), mo), device_id_type=MESH)
        greeted += 1
    for x in range(1, peers_mode):
        other = lax.rem(mo + x, peers_mode)
        pl.semaphore_signal(barrier, inc=1, device_id=(me, other), device_id_type=MESH)
        greeted += 1

    table[...] = (lax.broadcasted_iota(jnp.int32, (R, 128), 0) - 256).astype(F32).astype(BF16)
    loads[3].wait()
    ids = rows[...]
    off = jnp.bitwise_and(jnp.right_shift(ids, 12) - me + 2, subs - 1)
    off = jnp.where(ids < 0, -1, off)
    local = jnp.bitwise_and(ids, DOFS - 1)
    masks = jnp.concatenate([(off == o).astype(F32) for o in range(NOFF + 1)], axis=0)
    earlier = (
        lax.broadcasted_iota(jnp.int32, (CW, CW), 0) < lax.broadcasted_iota(jnp.int32, (CW, CW), 1)
    )
    ranks = mm(masks.astype(BF16), jnp.where(earlier, 1.0, 0.0).astype(BF16))
    totals = jnp.sum(masks, axis=1, keepdims=True)
    place = lax.broadcasted_iota(jnp.int32, (8, 1), 0)
    wanted = []
    for o in range(NOFF):
        count = totals[8 * o : 8 * o + 8]
        base = jnp.where(place >= 1, count[0:1], 0.0) + jnp.where(place >= 2, count[1:2], 0.0)
        rank = ranks[8 * o : 8 * o + 8] + base
        wanted.append(jnp.where(off == o, rank - SLOT // 2, 999.0))

    pl.semaphore_wait(barrier, greeted)

    for load in loads[:3]:
        load.wait()
    sends = []
    for n, x in enumerate((7, 6, 5, 4, 3, 2, 1)):
        sends.append((own3, own3, n, x))
    for n, x in enumerate((3, 2, 1)):
        sends.append((own2, own2, 7 + n, x))
    sends.append((own1, own1, 10, 1))
    sep_copies = [
        pltpu.make_async_remote_copy(
            src_ref=src,
            dst_ref=dst,
            send_sem=sep_send.at[n],
            recv_sem=sep_recv.at[n],
            device_id=(in_group(x), mo),
            device_id_type=MESH,
        )
        for src, dst, n, x in sends
    ]
    for copy in sep_copies:
        copy.start()

    values = jnp.concatenate(
        [
            jnp.right_shift(local, 6).astype(F32),
            jnp.bitwise_and(local, 63).astype(F32),
        ],
        axis=0,
    ).astype(BF16)
    for o in range(NOFF):
        parts = None
        for c in range(CLS):
            hit = one_hot(table[256 - SLOT // 2 : 256 + SLOT // 2], wanted[o][c : c + 1])
            pick[o, :, c * CW : (c + 1) * CW] = hit
            part = lax.dot_general(values, hit, (((1,), (1,)), ((), ())), preferred_element_type=F32)
            part = part[c : c + 1] * 64.0 + part[8 + c : 9 + c]
            parts = part if parts is None else parts + part
        lists[o] = parts.astype(jnp.int32)

    def list_copy(o, target):
        return pltpu.make_async_remote_copy(
            src_ref=lists.at[o],
            dst_ref=want.at[o],
            send_sem=list_send.at[o],
            recv_sem=list_recv.at[o],
            device_id=(target, mo),
            device_id_type=MESH,
        )

    far = (0, 1, 3, 4)
    list_copies = {o: list_copy(o, at_sub(o - 2)) for o in far}
    for o in far:
        list_copies[o].start()

    loads[4].wait()
    sep_copies[10].wait_recv()

    @pl.loop(0, NLEAF)
    def _(l):
        leaf_load(l).wait()
        cm_load(l).wait()
        x = jnp.concatenate([lc[l], a1[...]], axis=1)
        acc[l] = mm(x, w[l, 0 : KL + B, :])

    for n in range(7, 10):
        sep_copies[n].wait_recv()
    x23[:, 0:B] = jnp.transpose(a2[...])
    for n in range(7):
        sep_copies[n].wait_recv()
    x23[:, B : 2 * B] = jnp.transpose(a3[...])

    @pl.loop(0, NLEAF)
    def _(l):
        both = acc[l] + mm(x23[...], w[l, KL + B : KL + 3 * B, :])
        disp[:, pl.ds(pl.multiple_of(l * R, R), R)] = both.astype(BF16)

    def gather(o, wish, into):
        for l in range(NLEAF):
            here = jnp.right_shift(wish, 9) == l
            v = jnp.where(here, jnp.bitwise_and(wish, R - 1) - 256, 999).astype(F32)
            hot[l * R : (l + 1) * R, :] = one_hot(table[...], v)
        into[o] = mm(disp[...], hot[...]).astype(BF16)

    third = 3 - 2 * odd
    order = (0, 4, third, 4 - third)
    data_copies = []
    for o in order:
        list_copy(o, me).wait_recv()
        gather(o, want[o], gath)
        copy = pltpu.make_async_remote_copy(
            src_ref=gath.at[o],
            dst_ref=got.at[o],
            send_sem=data_send.at[o],
            recv_sem=data_recv.at[o],
            device_id=(at_sub(2 - o), mo),
            device_id_type=MESH,
        )
        copy.start()
        data_copies.append(copy)
    gather(2, lists[2], got)

    loads[7].wait()

    @pl.loop(0, NOFF)
    def _(o):
        for c in range(CLS):
            moved = mm(pick[o, :, c * CW : (c + 1) * CW], ops[c])
            perm[o, :, c * SR : (c + 1) * SR] = moved.astype(BF16)

    loads[5].wait()
    loads[6].wait()
    eye = lax.broadcasted_iota(jnp.int32, (MODES, MODES), 0) == lax.broadcasted_iota(
        jnp.int32, (MODES, MODES), 1
    )
    weight = jnp.sum(jnp.where(eye, mw[...], 0.0), axis=1, keepdims=True)

    def arrived(o):
        pltpu.make_async_remote_copy(
            src_ref=gath.at[o],
            dst_ref=got.at[o],
            send_sem=data_send.at[o],
            recv_sem=data_recv.at[o],
            device_id=(me, mo),
            device_id_type=MESH,
        ).wait_recv()

    sacc[...] = mm(got[2], perm[2])
    last = 4 - third
    for o in (0, 4, third):
        arrived(o)
        sacc[...] += mm(got[o], perm[o])
    arrived(last)
    energies = []
    for c in range(CLS):
        cols = slice(c * SR, (c + 1) * SR)
        s = sacc[:, cols] + mm(got[last], perm[last, :, cols])
        stress[c] = s
        e = jnp.sum(s * s * weight, axis=0, keepdims=True) * comp[c : c + 1]
        e = e[:, 0:128] + e[:, 128:256] + e[:, 256:384]
        energies.append((e + pltpu.roll(e, 64, 1)) * (0.5 / M))
    low = lax.broadcasted_iota(jnp.int32, (1, 128), 1) < 64
    mine = jnp.concatenate([jnp.where(low, energies[0], energies[1]), energies[2]], axis=1)
    terms[mo] = mine
    en_copies = []
    for x in range(1, peers_mode):
        other = lax.rem(mo + x, peers_mode)
        copy = pltpu.make_async_remote_copy(
            src_ref=terms.at[mo],
            dst_ref=terms.at[mo],
            send_sem=en_send.at[x],
            recv_sem=en_recv.at[x],
            device_id=(me, other),
            device_id_type=MESH,
        )
        copy.start()
        en_copies.append(copy)
    for copy in en_copies:
        copy.wait_recv()
    total = terms[0]
    for x in range(1, peers_mode):
        total = total + terms[x]
    share = CLS * 64 // peers_mode
    total = pltpu.roll(total, lax.rem(256 - share * mo, 256), 1)
    energy[...] = total[:, 0:share]

    for copy in sep_copies:
        copy.wait_send()
    for o in far:
        list_copies[o].wait_send()
    for copy in data_copies:
        copy.wait_send()
    for copy in en_copies:
        copy.wait_send()


def shards(lc, lm, cm, s1, s2, s3, rows, ops, comp, mw):
    subs = lax.axis_size("sub")
    peers_mode = lax.axis_size("mode")
    share = CLS * 64 // peers_mode
    anywhere = pl.BlockSpec(memory_space=pl.ANY)
    vmem = pl.BlockSpec(memory_space=pltpu.VMEM)
    dma = pltpu.SemaphoreType.DMA
    stress, energy = pl.pallas_call(
        functools.partial(kernel, subs, peers_mode),
        out_shape=(
            jax.ShapeDtypeStruct((CLS, MODES, SR), F32),
            jax.ShapeDtypeStruct((1, share), F32),
        ),
        in_specs=[anywhere] * 10,
        out_specs=(vmem, vmem),
        scratch_shapes=[
            pltpu.VMEM((NLEAF, MODES, KL), BF16),
            pltpu.VMEM((NLEAF, KL + 3 * B, R), BF16),
            pltpu.VMEM((MODES, B), BF16),
            pltpu.VMEM((B, MODES), BF16),
            pltpu.VMEM((B, MODES), BF16),
            pltpu.VMEM((MODES, 2 * B), BF16),
            pltpu.VMEM((8, CW), jnp.int32),
            pltpu.VMEM((CLS, CW, SR), BF16),
            pltpu.VMEM((CLS, SR), F32),
            pltpu.VMEM((1, MODES), F32),
            pltpu.VMEM((NLEAF, MODES, R), F32),
            pltpu.VMEM((MODES, DOFS), BF16),
            pltpu.VMEM((R, 128), BF16),
            pltpu.VMEM((NOFF, SLOT, CLS * CW), BF16),
            pltpu.VMEM((NOFF, SLOT, CLS * SR), BF16),
            pltpu.VMEM((NOFF, 1, SLOT), jnp.int32),
            pltpu.VMEM((NOFF, 1, SLOT), jnp.int32),
            pltpu.VMEM((DOFS, SLOT), BF16),
            pltpu.VMEM((NOFF, MODES, SLOT), BF16),
            pltpu.VMEM((NOFF, MODES, SLOT), BF16),
            pltpu.VMEM((MODES, CLS * SR), F32),
            pltpu.VMEM((peers_mode, 1, 256), F32),
            dma((8,)),
            dma((NLEAF,)),
            dma((NLEAF,)),
            dma((11,)),
            dma((11,)),
            dma((NOFF,)),
            dma((NOFF,)),
            dma((NOFF,)),
            dma((NOFF,)),
            dma((4,)),
            dma((4,)),
        ],
        compiler_params=pltpu.CompilerParams(
            collective_id=0, has_side_effects=True, vmem_limit_bytes=56 * 2**20
        ),
        name="back_transform",
    )(
        lc,
        lm,
        cm.reshape(NLEAF, 3 * B, R),
        s1,
        s2.T,
        s3.T,
        rows,
        ops,
        comp,
        mw.reshape(1, MODES),
    )
    return stress, energy.reshape(share)


def solution(mesh):
    return jax.shard_map(
        shards,
        mesh=mesh,
        in_specs=(
            P("sub", "mode", None),
            P("sub", None, None),
            P("sub", None, None, None),
            P("mode", "sub"),
            P("mode", "sub"),
            P("mode", "sub"),
            P("sub", None),
            P("sub", None, None),
            P("sub", None),
            P("mode"),
        ),
        out_specs=(P("sub", "mode", None), P(("sub", "mode"))),
        check_vma=False,
    )
```

```python
import functools

import jax
import jax.numpy as jnp
from jax import lax
from jax.experimental import pallas as pl
from jax.experimental.pallas import tpu as pltpu
from jax.sharding import PartitionSpec as P

M = 768
F32, BF16 = jnp.float32, jnp.bfloat16
MODES, NLEAF, KL, R, B = 192, 8, 128, 512, 256
DOFS = NLEAF * R
CLS, CW, SR = 3, 512, 384
SLOT, NOFF = 384, 5
MESH = pl.DeviceIdType.MESH


def mm(a, b):
    return jnp.dot(a, b, preferred_element_type=F32)


def one_hot(table, values):
    n, w = table.shape[0], values.shape[1]
    wide = jnp.broadcast_to(values, (16, w)).astype(BF16).reshape(1, 16, w)
    rows = jnp.concatenate([table.reshape(n // 16, 16, 128)] * (w // 128), axis=2)
    hit = rows == jnp.broadcast_to(wide, (n // 16, 16, w))
    return jnp.where(hit, jnp.ones((), BF16), jnp.zeros((), BF16)).reshape(n, w)


def kernel(
    subs,
    peers_mode,
    lc_h,
    lm_h,
    cm_h,
    s1_h,
    s2_h,
    s3_h,
    rows_h,
    ops_h,
    comp_h,
    mw_h,
    cols_h,
    energy,
    lc,
    w,
    a1,
    a2,
    a3,
    x23,
    rows,
    ops,
    comp,
    mw,
    acc,
    disp,
    table,
    pick,
    lists,
    want,
    hot,
    own_hot,
    gath,
    got,
    cols32,
    cols,
    terms,
    in_sem,
    leaf_sem,
    cm_sem,
    sep_send,
    sep_recv,
    list_send,
    list_recv,
    data_send,
    data_recv,
    en_send,
    en_recv,
):
    me = lax.axis_index("sub")
    mo = lax.axis_index("mode")
    odd = lax.rem(me, 2)
    in_eight = lax.rem(me, 8)
    in_four = lax.rem(me, 4)

    def at_sub(offset):
        return lax.rem(me + offset + subs, subs)

    def in_group(x):
        return me - in_eight + jnp.bitwise_xor(in_eight, x)

    barrier = pltpu.get_barrier_semaphore()
    greeted = 0
    for x in range(1, 8):
        pl.semaphore_signal(barrier, inc=1, device_id=(in_group(x), mo), device_id_type=MESH)
        greeted += 1
    for q in (-2, -1, 1, 2):
        pl.semaphore_signal(barrier, inc=1, device_id=(at_sub(q), mo), device_id_type=MESH)
        greeted += 1
    for x in range(1, peers_mode):
        other = lax.rem(mo + x, peers_mode)
        pl.semaphore_signal(barrier, inc=1, device_id=(me, other), device_id_type=MESH)
        greeted += 1

    rows[...] = jnp.full(rows.shape, -1, jnp.int32)
    own1 = a1.at[:, pl.ds(pl.multiple_of(odd * 128, 128), 128)]
    own2 = a2.at[pl.ds(pl.multiple_of(in_four * 64, 64), 64), :]
    own3 = a3.at[pl.ds(pl.multiple_of(in_eight * 32, 32), 32), :]
    loads = [
        pltpu.make_async_copy(rows_h, rows.at[pl.ds(0, CLS), :], in_sem.at[0]),
        pltpu.make_async_copy(s3_h, own3, in_sem.at[1]),
        pltpu.make_async_copy(s2_h, own2, in_sem.at[2]),
        pltpu.make_async_copy(s1_h, own1, in_sem.at[3]),
        pltpu.make_async_copy(lc_h, lc, in_sem.at[4]),
        pltpu.make_async_copy(comp_h, comp, in_sem.at[5]),
        pltpu.make_async_copy(mw_h, mw, in_sem.at[6]),
        pltpu.make_async_copy(ops_h, ops, in_sem.at[7]),
    ]
    for load in loads[:4]:
        load.start()
    pl.semaphore_wait(barrier, greeted)

    sends = [(s3_h, own3, n, x) for n, x in enumerate((7, 6, 5, 4, 3, 2, 1))]
    sends += [(s2_h, own2, 7 + n, x) for n, x in enumerate((3, 2, 1))]
    sends.append((s1_h, own1, 10, 1))
    sep_copies = [
        pltpu.make_async_remote_copy(
            src_ref=src,
            dst_ref=dst,
            send_sem=sep_send.at[n],
            recv_sem=sep_recv.at[n],
            device_id=(in_group(x), mo),
            device_id_type=MESH,
        )
        for src, dst, n, x in sends
    ]
    for copy in sep_copies:
        copy.start()

    def leaf_load(l):
        return pltpu.make_async_copy(lm_h.at[l], w.at[l, pl.ds(0, KL), :], leaf_sem.at[l])

    def cm_load(l):
        return pltpu.make_async_copy(cm_h.at[l], w.at[l, pl.ds(KL, 3 * B), :], cm_sem.at[l])

    loads[4].start()
    for l in range(NLEAF):
        leaf_load(l).start()
        cm_load(l).start()
    for load in loads[5:]:
        load.start()

    table[...] = (lax.broadcasted_iota(jnp.int32, (R, 128), 0) - 256).astype(F32).astype(BF16)
    earlier = (
        lax.broadcasted_iota(jnp.int32, (CW, CW), 0) < lax.broadcasted_iota(jnp.int32, (CW, CW), 1)
    )
    earlier = jnp.where(earlier, 1.0, 0.0).astype(BF16)
    loads[0].wait()
    ids = rows[...]
    off = jnp.bitwise_and(jnp.right_shift(ids, 12) - me + 2, subs - 1)
    off = jnp.where(ids < 0, -1, off)
    local = jnp.bitwise_and(ids, DOFS - 1)
    masks = jnp.concatenate([(off == o).astype(F32) for o in range(NOFF + 1)], axis=0)
    ranks = mm(masks.astype(BF16), earlier)
    totals = jnp.sum(masks, axis=1, keepdims=True)
    line = lax.broadcasted_iota(jnp.int32, (8, 1), 0)
    wanted = []
    slot = jnp.full((8, CW), -1, jnp.int32)
    for o in range(NOFF):
        count = totals[8 * o : 8 * o + 8]
        base = jnp.where(line >= 1, count[0:1], 0.0) + jnp.where(line >= 2, count[1:2], 0.0)
        rank = ranks[8 * o : 8 * o + 8] + base
        wanted.append(jnp.where(off == o, rank - SLOT // 2, 999.0))
        slot = jnp.where(off == o, rank.astype(jnp.int32) + SLOT * o, slot)
    slot_row, slot_col = jnp.right_shift(slot, 7), jnp.bitwise_and(slot, 127)
    high, low = jnp.right_shift(local, 6), jnp.bitwise_and(local, 63)
    sixteen = lax.broadcasted_iota(jnp.int32, (16, CW), 0)
    left, right = [], []
    for c in range(CLS):
        here = slot_row[c : c + 1] == sixteen
        both = [jnp.where(here, part[c : c + 1], 0) for part in (high, low)]
        left.append(jnp.concatenate(both, axis=0).astype(F32).astype(BF16))
        right.append(one_hot(table[256:384], slot_col[c : c + 1].astype(F32)))
    found = lax.dot_general(
        jnp.concatenate(left, axis=1),
        jnp.concatenate(right, axis=1),
        (((1,), (1,)), ((), ())),
        preferred_element_type=F32,
    )
    found = (found[0:16] * 64.0 + found[16:32]).astype(jnp.int32)
    for r in range(3 * NOFF):
        lists[r] = found[r : r + 1]

    def list_copy(o, target):
        return pltpu.make_async_remote_copy(
            src_ref=lists.at[pl.ds(3 * o, 3)],
            dst_ref=want.at[pl.ds(3 * o, 3)],
            send_sem=list_send.at[o],
            recv_sem=list_recv.at[o],
            device_id=(target, mo),
            device_id_type=MESH,
        )

    far = (0, 4, 1, 3)
    list_copies = [list_copy(o, at_sub(o - 2)) for o in far]
    for copy in list_copies:
        copy.start()

    loads[3].wait()
    loads[4].wait()
    sep_copies[10].wait_recv()
    for l in range(NLEAF):
        leaf_load(l).wait()
        cm_load(l).wait()
        x = jnp.concatenate([lc[l], a1[...]], axis=1)
        acc[l] = mm(x, w[l, 0 : KL + B, :])

    for o in range(NOFF):
        for c in range(CLS):
            hit = one_hot(table[256 - SLOT // 2 : 256 + SLOT // 2], wanted[o][c : c + 1])
            pick[o, :, c * CW : (c + 1) * CW] = hit

    loads[2].wait()
    for n in range(7, 10):
        sep_copies[n].wait_recv()
    x23[:, 0:B] = jnp.transpose(a2[...])
    loads[1].wait()
    for n in range(7):
        sep_copies[n].wait_recv()
    x23[:, B : 2 * B] = jnp.transpose(a3[...])
    for l in range(NLEAF):
        both = acc[l] + mm(x23[...], w[l, KL + B : KL + 3 * B, :])
        disp[:, l * R : (l + 1) * R] = both.astype(BF16)

    def hot_rows(wish, into):
        for l in range(NLEAF):
            here = jnp.right_shift(wish, 9) == l
            v = jnp.where(here, jnp.bitwise_and(wish, R - 1) - 256, 999).astype(F32)
            into[l * R : (l + 1) * R, :] = one_hot(table[...], v)

    third = 3 - 2 * odd
    fourth = 4 - third

    def data_copy(r, target):
        return pltpu.make_async_remote_copy(
            src_ref=gath.at[r],
            dst_ref=got.at[r],
            send_sem=data_send.at[r],
            recv_sem=data_recv.at[r],
            device_id=(target, mo),
            device_id_type=MESH,
        )

    for copy in list_copies:
        copy.wait_recv()

    @pl.loop(0, 6)
    def _(t):
        late = t // 3
        part = lax.rem(t, 3)
        o1 = late * third
        o2 = 4 - o1
        r1, r2 = 3 * o1 + part, 3 * o2 + part
        hot_rows(jnp.concatenate([want[r1], want[r2]], axis=1), hot)
        both = mm(disp[...], hot[...]).astype(BF16)
        gath[r1] = both[:, 0:128]
        data_copy(r1, at_sub(2 - o1)).start()
        gath[r2] = both[:, 128:256]
        data_copy(r2, at_sub(2 - o2)).start()

    hot_rows(jnp.concatenate([lists[6], lists[7], lists[8]], axis=1), own_hot)
    own = mm(disp[...], own_hot[...]).astype(BF16)

    def arrived(o):
        for part in range(3):
            data_copy(3 * o + part, me).wait_recv()
        return [got[3 * o + part] for part in range(3)]

    x = jnp.concatenate([own] + arrived(third), axis=1)
    rhs = jnp.concatenate([pick[2], pick[third]], axis=0)
    cols32[...] = mm(x, rhs)
    x = jnp.concatenate(arrived(0) + arrived(4), axis=1)
    cols32[...] += mm(x, jnp.concatenate([pick[0], pick[4]], axis=0))
    for load in loads[5:]:
        load.wait()
    eye = lax.broadcasted_iota(jnp.int32, (MODES, MODES), 0) == lax.broadcasted_iota(
        jnp.int32, (MODES, MODES), 1
    )
    weight = jnp.sum(jnp.where(eye, mw[...], 0.0), axis=1, keepdims=True)
    x = jnp.concatenate(arrived(fourth), axis=1)
    cols[...] = (cols32[...] + mm(x, pick[fourth])).astype(BF16)
    out = pltpu.make_async_copy(cols, cols_h, in_sem.at[8])
    out.start()

    energies = []
    for c in range(CLS):
        s = mm(cols[:, c * CW : (c + 1) * CW], ops[c])
        e = jnp.sum(s * s * weight, axis=0, keepdims=True) * comp[c : c + 1]
        e = e[:, 0:128] + e[:, 128:256] + e[:, 256:384]
        energies.append((e + pltpu.roll(e, 64, 1)) * (0.5 / M))
    half = lax.broadcasted_iota(jnp.int32, (1, 128), 1) < 64
    terms[mo] = jnp.concatenate([jnp.where(half, energies[0], energies[1]), energies[2]], axis=1)
    en_copies = []
    for x in range(1, peers_mode):
        other = lax.rem(mo + x, peers_mode)
        copy = pltpu.make_async_remote_copy(
            src_ref=terms.at[mo],
            dst_ref=terms.at[mo],
            send_sem=en_send.at[x],
            recv_sem=en_recv.at[x],
            device_id=(me, other),
            device_id_type=MESH,
        )
        copy.start()
        en_copies.append(copy)

    for copy in sep_copies:
        copy.wait_send()
    for copy in list_copies:
        copy.wait_send()
    for o in far:
        for part in range(3):
            data_copy(3 * o + part, me).wait_send()
    for copy in en_copies:
        copy.wait_recv()
    total = terms[0]
    for x in range(1, peers_mode):
        total = total + terms[x]
    share = CLS * 64 // peers_mode
    total = pltpu.roll(total, lax.rem(256 - share * mo, 256), 1)
    energy[...] = total[:, 0:share]
    for copy in en_copies:
        copy.wait_send()
    out.wait()


def stress_kernel(cols_h, ops, sums_h, stress_h, energy_h, cols, stress, in_sem, out_sem):
    pass_on = pltpu.make_async_copy(sums_h, energy_h, out_sem.at[CLS])
    pass_on.start()
    loads = []
    for c in range(CLS):
        piece = pl.ds(c * CW, CW)
        loads.append(pltpu.make_async_copy(cols_h.at[:, piece], cols.at[:, piece], in_sem.at[c]))
        loads[c].start()
    stores = []
    for c in range(CLS):
        loads[c].wait()
        stress[c] = mm(cols[:, c * CW : (c + 1) * CW], ops[c])
        stores.append(pltpu.make_async_copy(stress.at[c], stress_h.at[c], out_sem.at[c]))
        stores[c].start()
    for store in stores:
        store.wait()
    pass_on.wait()


def shards(lc, lm, cm, s1, s2, s3, rows, ops, comp, mw):
    subs = lax.axis_size("sub")
    peers_mode = lax.axis_size("mode")
    share = CLS * 64 // peers_mode
    anywhere = pl.BlockSpec(memory_space=pl.ANY)
    vmem = pl.BlockSpec(memory_space=pltpu.VMEM)
    hbm = pl.BlockSpec(memory_space=pltpu.HBM)
    dma = pltpu.SemaphoreType.DMA
    cols, sums = pl.pallas_call(
        functools.partial(kernel, subs, peers_mode),
        out_shape=(
            jax.ShapeDtypeStruct((MODES, CLS * CW), BF16),
            jax.ShapeDtypeStruct((1, share), F32),
        ),
        in_specs=[anywhere] * 10,
        out_specs=(anywhere, vmem),
        scratch_shapes=[
            pltpu.VMEM((NLEAF, MODES, KL), BF16),
            pltpu.VMEM((NLEAF, KL + 3 * B, R), BF16),
            pltpu.VMEM((MODES, B), BF16),
            pltpu.VMEM((B, MODES), BF16),
            pltpu.VMEM((B, MODES), BF16),
            pltpu.VMEM((MODES, 2 * B), BF16),
            pltpu.VMEM((8, CW), jnp.int32),
            pltpu.VMEM((CLS, CW, SR), BF16),
            pltpu.VMEM((CLS, SR), F32),
            pltpu.VMEM((1, MODES), F32),
            pltpu.VMEM((NLEAF, MODES, R), F32),
            pltpu.VMEM((MODES, DOFS), BF16),
            pltpu.VMEM((R, 128), BF16),
            pltpu.VMEM((NOFF, SLOT, CLS * CW), BF16),
            pltpu.VMEM((3 * NOFF, 1, 128), jnp.int32),
            pltpu.VMEM((3 * NOFF, 1, 128), jnp.int32),
            pltpu.VMEM((DOFS, 256), BF16),
            pltpu.VMEM((DOFS, SLOT), BF16),
            pltpu.VMEM((3 * NOFF, MODES, 128), BF16),
            pltpu.VMEM((3 * NOFF, MODES, 128), BF16),
            pltpu.VMEM((MODES, CLS * CW), F32),
            pltpu.VMEM((MODES, CLS * CW), BF16),
            pltpu.VMEM((peers_mode, 1, 256), F32),
            dma((9,)),
            dma((NLEAF,)),
            dma((NLEAF,)),
            dma((11,)),
            dma((11,)),
            dma((NOFF,)),
            dma((NOFF,)),
            dma((3 * NOFF,)),
            dma((3 * NOFF,)),
            dma((4,)),
            dma((4,)),
        ],
        compiler_params=pltpu.CompilerParams(
            collective_id=0, has_side_effects=True, vmem_limit_bytes=40 * 2**20
        ),
        name="back_transform",
    )(
        lc,
        lm,
        cm.reshape(NLEAF, 3 * B, R),
        s1,
        s2.T,
        s3.T,
        rows,
        ops,
        comp,
        mw.reshape(1, MODES),
    )
    stress, energy = pl.pallas_call(
        stress_kernel,
        out_shape=(
            jax.ShapeDtypeStruct((CLS, MODES, SR), F32),
            jax.ShapeDtypeStruct((1, share), F32),
        ),
        in_specs=[hbm, vmem, hbm],
        out_specs=(anywhere, anywhere),
        scratch_shapes=[
            pltpu.VMEM((MODES, CLS * CW), BF16),
            pltpu.VMEM((CLS, MODES, SR), F32),
            dma((CLS,)),
            dma((CLS + 1,)),
        ],
        compiler_params=pltpu.CompilerParams(vmem_limit_bytes=16 * 2**20),
        name="stress_rows",
    )(cols, ops, sums)
    return stress, energy.reshape(share)


def solution(mesh):
    return jax.shard_map(
        shards,
        mesh=mesh,
        in_specs=(
            P("sub", "mode", None),
            P("sub", None, None),
            P("sub", None, None, None),
            P("mode", "sub"),
            P("mode", "sub"),
            P("mode", "sub"),
            P("sub", None),
            P("sub", None, None),
            P("sub", None),
            P("mode"),
        ),
        out_specs=(P("sub", "mode", None), P(("sub", "mode"))),
        check_vma=False,
    )
```

```python
import functools

import jax
import jax.numpy as jnp
from jax import lax
from jax.experimental import pallas as pl
from jax.experimental.pallas import tpu as pltpu
from jax.sharding import PartitionSpec as P

M = 768
F32, BF16 = jnp.float32, jnp.bfloat16
MODES, NLEAF, KL, R, B = 192, 8, 128, 512, 256
DOFS = NLEAF * R
CLS, CW, SR = 3, 512, 384
SLOT, NOFF = 384, 5
MESH = pl.DeviceIdType.MESH


def mm(a, b):
    return jnp.dot(a, b, preferred_element_type=F32)


def one_hot(table, values):
    n, w = table.shape[0], values.shape[1]
    wide = jnp.broadcast_to(values, (16, w)).astype(BF16).reshape(1, 16, w)
    rows = jnp.concatenate([table.reshape(n // 16, 16, 128)] * (w // 128), axis=2)
    hit = rows == jnp.broadcast_to(wide, (n // 16, 16, w))
    return jnp.where(hit, jnp.ones((), BF16), jnp.zeros((), BF16)).reshape(n, w)


def kernel(
    subs,
    peers_mode,
    lc_h,
    lm_h,
    cm_h,
    s1_h,
    s2_h,
    s3_h,
    rows_h,
    ops_h,
    comp_h,
    mw_h,
    stress,
    energy,
    lc,
    w,
    a1,
    a2,
    a3,
    x23,
    rows,
    ops,
    comp,
    mw,
    acc,
    disp,
    table,
    pick,
    lists,
    want,
    hot,
    own_hot,
    gath,
    got,
    cols32,
    cols,
    terms,
    in_sem,
    leaf_sem,
    cm_sem,
    sep_send,
    sep_recv,
    list_send,
    list_recv,
    data_send,
    data_recv,
    en_send,
    en_recv,
):
    me = lax.axis_index("sub")
    mo = lax.axis_index("mode")
    odd = lax.rem(me, 2)
    in_eight = lax.rem(me, 8)
    in_four = lax.rem(me, 4)

    def at_sub(offset):
        return lax.rem(me + offset + subs, subs)

    def in_group(x):
        return me - in_eight + jnp.bitwise_xor(in_eight, x)

    barrier = pltpu.get_barrier_semaphore()
    greeted = 0
    for x in range(1, 8):
        pl.semaphore_signal(barrier, inc=1, device_id=(in_group(x), mo), device_id_type=MESH)
        greeted += 1
    for q in (-2, -1, 1, 2):
        pl.semaphore_signal(barrier, inc=1, device_id=(at_sub(q), mo), device_id_type=MESH)
        greeted += 1
    for x in range(1, peers_mode):
        other = lax.rem(mo + x, peers_mode)
        pl.semaphore_signal(barrier, inc=1, device_id=(me, other), device_id_type=MESH)
        greeted += 1

    rows[...] = jnp.full(rows.shape, -1, jnp.int32)
    own1 = a1.at[:, pl.ds(pl.multiple_of(odd * 128, 128), 128)]
    own2 = a2.at[pl.ds(pl.multiple_of(in_four * 64, 64), 64), :]
    own3 = a3.at[pl.ds(pl.multiple_of(in_eight * 32, 32), 32), :]
    loads = [
        pltpu.make_async_copy(rows_h, rows.at[pl.ds(0, CLS), :], in_sem.at[0]),
        pltpu.make_async_copy(s3_h, own3, in_sem.at[1]),
        pltpu.make_async_copy(s2_h, own2, in_sem.at[2]),
        pltpu.make_async_copy(s1_h, own1, in_sem.at[3]),
        pltpu.make_async_copy(lc_h, lc, in_sem.at[4]),
        pltpu.make_async_copy(comp_h, comp, in_sem.at[5]),
        pltpu.make_async_copy(mw_h, mw, in_sem.at[6]),
        pltpu.make_async_copy(ops_h, ops, in_sem.at[7]),
    ]
    for load in loads[:4]:
        load.start()
    pl.semaphore_wait(barrier, greeted)

    sends = [(s1_h, own1, 10, 1)]
    sends += [(s2_h, own2, 7 + n, x) for n, x in enumerate((3, 2, 1))]
    sends += [(s3_h, own3, n, x) for n, x in enumerate((7, 6, 5, 4, 3, 2, 1))]
    sep_copies = [
        pltpu.make_async_remote_copy(
            src_ref=src,
            dst_ref=dst,
            send_sem=sep_send.at[n],
            recv_sem=sep_recv.at[n],
            device_id=(in_group(x), mo),
            device_id_type=MESH,
        )
        for src, dst, n, x in sends
    ]
    for copy in sep_copies:
        copy.start()

    def leaf_load(l):
        return pltpu.make_async_copy(lm_h.at[l], w.at[l, pl.ds(0, KL), :], leaf_sem.at[l])

    def cm_load(l):
        return pltpu.make_async_copy(cm_h.at[l], w.at[l, pl.ds(KL, 3 * B), :], cm_sem.at[l])

    loads[4].start()
    for l in range(NLEAF):
        leaf_load(l).start()
        cm_load(l).start()
    for load in loads[5:]:
        load.start()

    table[...] = (lax.broadcasted_iota(jnp.int32, (R, 128), 0) - 256).astype(F32).astype(BF16)
    earlier = (
        lax.broadcasted_iota(jnp.int32, (CW, CW), 0) < lax.broadcasted_iota(jnp.int32, (CW, CW), 1)
    )
    earlier = jnp.where(earlier, 1.0, 0.0).astype(BF16)
    loads[0].wait()
    ids = rows[...]
    off = jnp.bitwise_and(jnp.right_shift(ids, 12) - me + 2, subs - 1)
    off = jnp.where(ids < 0, -1, off)
    local = jnp.bitwise_and(ids, DOFS - 1)
    masks = jnp.concatenate([(off == o).astype(F32) for o in range(NOFF + 1)], axis=0)
    ranks = mm(masks.astype(BF16), earlier)
    totals = jnp.sum(masks, axis=1, keepdims=True)
    line = lax.broadcasted_iota(jnp.int32, (8, 1), 0)
    wanted = []
    slot = jnp.full((8, CW), -1, jnp.int32)
    for o in range(NOFF):
        count = totals[8 * o : 8 * o + 8]
        base = jnp.where(line >= 1, count[0:1], 0.0) + jnp.where(line >= 2, count[1:2], 0.0)
        rank = ranks[8 * o : 8 * o + 8] + base
        wanted.append(jnp.where(off == o, rank - SLOT // 2, 999.0))
        slot = jnp.where(off == o, rank.astype(jnp.int32) + SLOT * o, slot)
    slot_row, slot_col = jnp.right_shift(slot, 7), jnp.bitwise_and(slot, 127)
    high, low = jnp.right_shift(local, 6), jnp.bitwise_and(local, 63)
    sixteen = lax.broadcasted_iota(jnp.int32, (16, CW), 0)
    left, right = [], []
    for c in range(CLS):
        here = slot_row[c : c + 1] == sixteen
        both = [jnp.where(here, part[c : c + 1], 0) for part in (high, low)]
        left.append(jnp.concatenate(both, axis=0).astype(F32).astype(BF16))
        right.append(one_hot(table[256:384], slot_col[c : c + 1].astype(F32)))
    found = lax.dot_general(
        jnp.concatenate(left, axis=1),
        jnp.concatenate(right, axis=1),
        (((1,), (1,)), ((), ())),
        preferred_element_type=F32,
    )
    found = (found[0:16] * 64.0 + found[16:32]).astype(jnp.int32)
    for r in range(3 * NOFF):
        lists[r] = found[r : r + 1]

    def list_copy(o, target):
        return pltpu.make_async_remote_copy(
            src_ref=lists.at[pl.ds(3 * o, 3)],
            dst_ref=want.at[pl.ds(3 * o, 3)],
            send_sem=list_send.at[o],
            recv_sem=list_recv.at[o],
            device_id=(target, mo),
            device_id_type=MESH,
        )

    far = (0, 4, 1, 3)
    list_copies = [list_copy(o, at_sub(o - 2)) for o in far]
    for copy in list_copies:
        copy.start()

    for o in range(NOFF):
        for c in range(CLS):
            hit = one_hot(table[256 - SLOT // 2 : 256 + SLOT // 2], wanted[o][c : c + 1])
            pick[o, :, c * CW : (c + 1) * CW] = hit

    for load in loads[2:5]:
        load.wait()
    for copy in sep_copies[0:4]:
        copy.wait_recv()
    x23[:, 0:B] = jnp.transpose(a2[...])
    for l in range(NLEAF):
        leaf_load(l).wait()
        cm_load(l).wait()
        x = jnp.concatenate([lc[l], a1[...], x23[:, 0:B]], axis=1)
        acc[l] = mm(x, w[l, 0 : KL + 2 * B, :])
    loads[1].wait()
    for copy in sep_copies[4:]:
        copy.wait_recv()
    x23[:, B : 2 * B] = jnp.transpose(a3[...])
    for l in range(NLEAF):
        both = acc[l] + mm(x23[:, B : 2 * B], w[l, KL + 2 * B : KL + 3 * B, :])
        disp[:, l * R : (l + 1) * R] = both.astype(BF16)

    def hot_rows(wish, into):
        for l in range(NLEAF):
            here = jnp.right_shift(wish, 9) == l
            v = jnp.where(here, jnp.bitwise_and(wish, R - 1) - 256, 999).astype(F32)
            into[l * R : (l + 1) * R, :] = one_hot(table[...], v)

    third = 3 - 2 * odd
    fourth = 4 - third

    def data_copy(r, target):
        return pltpu.make_async_remote_copy(
            src_ref=gath.at[r],
            dst_ref=got.at[r],
            send_sem=data_send.at[r],
            recv_sem=data_recv.at[r],
            device_id=(target, mo),
            device_id_type=MESH,
        )

    for copy in list_copies:
        copy.wait_recv()

    @pl.loop(0, 6)
    def _(t):
        late = t // 3
        part = lax.rem(t, 3)
        o1 = late * third
        o2 = 4 - o1
        r1, r2 = 3 * o1 + part, 3 * o2 + part
        hot_rows(jnp.concatenate([want[r1], want[r2]], axis=1), hot)
        both = mm(disp[...], hot[...]).astype(BF16)
        gath[r1] = both[:, 0:128]
        data_copy(r1, at_sub(2 - o1)).start()
        gath[r2] = both[:, 128:256]
        data_copy(r2, at_sub(2 - o2)).start()

    hot_rows(jnp.concatenate([lists[6], lists[7], lists[8]], axis=1), own_hot)
    own = mm(disp[...], own_hot[...]).astype(BF16)

    def arrived(o):
        for part in range(3):
            data_copy(3 * o + part, me).wait_recv()
        return [got[3 * o + part] for part in range(3)]

    x = jnp.concatenate([own] + arrived(third), axis=1)
    rhs = jnp.concatenate([pick[2], pick[third]], axis=0)
    cols32[...] = mm(x, rhs)
    x = jnp.concatenate(arrived(0) + arrived(4), axis=1)
    cols32[...] += mm(x, jnp.concatenate([pick[0], pick[4]], axis=0))
    for load in loads[5:]:
        load.wait()
    eye = lax.broadcasted_iota(jnp.int32, (MODES, MODES), 0) == lax.broadcasted_iota(
        jnp.int32, (MODES, MODES), 1
    )
    weight = jnp.sum(jnp.where(eye, mw[...], 0.0), axis=1, keepdims=True)
    x = jnp.concatenate(arrived(fourth), axis=1)
    cols[...] = (cols32[...] + mm(x, pick[fourth])).astype(BF16)
    energies = []
    for c in range(CLS):
        s = mm(cols[:, c * CW : (c + 1) * CW], ops[c])
        stress[c] = s
        e = jnp.sum(s * s * weight, axis=0, keepdims=True) * comp[c : c + 1]
        e = e[:, 0:128] + e[:, 128:256] + e[:, 256:384]
        energies.append((e + pltpu.roll(e, 64, 1)) * (0.5 / M))
    half = lax.broadcasted_iota(jnp.int32, (1, 128), 1) < 64
    terms[mo] = jnp.concatenate([jnp.where(half, energies[0], energies[1]), energies[2]], axis=1)
    en_copies = []
    for x in range(1, peers_mode):
        other = lax.rem(mo + x, peers_mode)
        copy = pltpu.make_async_remote_copy(
            src_ref=terms.at[mo],
            dst_ref=terms.at[mo],
            send_sem=en_send.at[x],
            recv_sem=en_recv.at[x],
            device_id=(me, other),
            device_id_type=MESH,
        )
        copy.start()
        en_copies.append(copy)

    for copy in sep_copies:
        copy.wait_send()
    for copy in list_copies:
        copy.wait_send()
    for o in far:
        for part in range(3):
            data_copy(3 * o + part, me).wait_send()
    for copy in en_copies:
        copy.wait_recv()
    total = terms[0]
    for x in range(1, peers_mode):
        total = total + terms[x]
    share = CLS * 64 // peers_mode
    total = pltpu.roll(total, lax.rem(256 - share * mo, 256), 1)
    energy[...] = total[:, 0:share]
    for copy in en_copies:
        copy.wait_send()


def hand_out(stress_v, energy_v, stress_h, energy_h, sem):
    copies = [pltpu.make_async_copy(energy_v, energy_h, sem.at[CLS])]
    for c in range(CLS):
        copies.append(pltpu.make_async_copy(stress_v.at[c], stress_h.at[c], sem.at[c]))
    for copy in copies:
        copy.start()
    for copy in copies:
        copy.wait()


def shards(lc, lm, cm, s1, s2, s3, rows, ops, comp, mw):
    subs = lax.axis_size("sub")
    peers_mode = lax.axis_size("mode")
    share = CLS * 64 // peers_mode
    anywhere = pl.BlockSpec(memory_space=pl.ANY)
    vmem = pl.BlockSpec(memory_space=pltpu.VMEM)
    dma = pltpu.SemaphoreType.DMA
    values = (
        lc,
        lm,
        cm.reshape(NLEAF, 3 * B, R),
        s1,
        s2.T,
        s3.T,
        rows,
        ops,
        comp,
        mw.reshape(1, MODES),
    )
    stress, energy = pl.pallas_call(
        functools.partial(kernel, subs, peers_mode),
        out_shape=(
            pltpu.VMEM((CLS, MODES, SR), F32),
            pltpu.VMEM((1, share), F32),
        ),
        in_specs=[anywhere] * 10,
        out_specs=(vmem, vmem),
        scratch_shapes=[
            pltpu.VMEM((NLEAF, MODES, KL), BF16),
            pltpu.VMEM((NLEAF, KL + 3 * B, R), BF16),
            pltpu.VMEM((MODES, B), BF16),
            pltpu.VMEM((B, MODES), BF16),
            pltpu.VMEM((B, MODES), BF16),
            pltpu.VMEM((MODES, 2 * B), BF16),
            pltpu.VMEM((8, CW), jnp.int32),
            pltpu.VMEM((CLS, CW, SR), BF16),
            pltpu.VMEM((CLS, SR), F32),
            pltpu.VMEM((1, MODES), F32),
            pltpu.VMEM((NLEAF, MODES, R), F32),
            pltpu.VMEM((MODES, DOFS), BF16),
            pltpu.VMEM((R, 128), BF16),
            pltpu.VMEM((NOFF, SLOT, CLS * CW), BF16),
            pltpu.VMEM((3 * NOFF, 1, 128), jnp.int32),
            pltpu.VMEM((3 * NOFF, 1, 128), jnp.int32),
            pltpu.VMEM((DOFS, 256), BF16),
            pltpu.VMEM((DOFS, SLOT), BF16),
            pltpu.VMEM((3 * NOFF, MODES, 128), BF16),
            pltpu.VMEM((3 * NOFF, MODES, 128), BF16),
            pltpu.VMEM((MODES, CLS * CW), F32),
            pltpu.VMEM((MODES, CLS * CW), BF16),
            pltpu.VMEM((peers_mode, 1, 256), F32),
            dma((8,)),
            dma((NLEAF,)),
            dma((NLEAF,)),
            dma((11,)),
            dma((11,)),
            dma((NOFF,)),
            dma((NOFF,)),
            dma((3 * NOFF,)),
            dma((3 * NOFF,)),
            dma((4,)),
            dma((4,)),
        ],
        compiler_params=pltpu.CompilerParams(
            collective_id=0, has_side_effects=True, vmem_limit_bytes=44 * 2**20
        ),
        name="back_transform",
    )(*[pltpu.with_memory_space_constraint(value, pltpu.HBM) for value in values])
    stress, energy = pl.pallas_call(
        hand_out,
        out_shape=(
            jax.ShapeDtypeStruct((CLS, MODES, SR), F32),
            jax.ShapeDtypeStruct((1, share), F32),
        ),
        in_specs=[anywhere] * 2,
        out_specs=(anywhere, anywhere),
        scratch_shapes=[dma((CLS + 1,))],
        compiler_params=pltpu.CompilerParams(vmem_limit_bytes=16 * 2**20),
        name="hand_out",
    )(stress, energy)
    return stress, energy.reshape(share)


def solution(mesh):
    return jax.shard_map(
        shards,
        mesh=mesh,
        in_specs=(
            P("sub", "mode", None),
            P("sub", None, None),
            P("sub", None, None, None),
            P("mode", "sub"),
            P("mode", "sub"),
            P("mode", "sub"),
            P("sub", None),
            P("sub", None, None),
            P("sub", None),
            P("mode"),
        ),
        out_specs=(P("sub", "mode", None), P(("sub", "mode"))),
        check_vma=False,
    )
```

```python
import functools

import jax
import jax.numpy as jnp
from jax import lax
from jax.experimental import pallas as pl
from jax.experimental.pallas import tpu as pltpu
from jax.sharding import PartitionSpec as P

M = 768
F32, BF16 = jnp.float32, jnp.bfloat16
MODES, NLEAF, KL, R, B = 192, 8, 128, 512, 256
DOFS = NLEAF * R
CLS, CW, SR = 3, 512, 384
SLOT, NOFF = 384, 5
MESH = pl.DeviceIdType.MESH


def mm(a, b):
    return jnp.dot(a, b, preferred_element_type=F32)


def one_hot(table, values):
    n, w = table.shape[0], values.shape[1]
    wide = jnp.broadcast_to(values, (16, w)).astype(BF16).reshape(1, 16, w)
    rows = jnp.concatenate([table.reshape(n // 16, 16, 128)] * (w // 128), axis=2)
    hit = rows == jnp.broadcast_to(wide, (n // 16, 16, w))
    return jnp.where(hit, jnp.ones((), BF16), jnp.zeros((), BF16)).reshape(n, w)


def kernel(
    subs,
    peers_mode,
    lc_h,
    lm_h,
    cm_h,
    s1_h,
    s2_h,
    s3_h,
    rows_h,
    ops_h,
    comp_h,
    mw_h,
    stress,
    energy,
    lc,
    w,
    a1,
    a2,
    a3,
    x23,
    rows,
    ops,
    comp,
    mw,
    acc,
    disp,
    table,
    pick,
    lists,
    want,
    hot,
    own_hot,
    gath,
    got,
    cols32,
    cols,
    terms,
    in_sem,
    leaf_sem,
    cm_sem,
    sep_send,
    sep_recv,
    list_send,
    list_recv,
    data_send,
    data_recv,
    en_send,
    en_recv,
):
    me = lax.axis_index("sub")
    mo = lax.axis_index("mode")
    odd = lax.rem(me, 2)
    in_eight = lax.rem(me, 8)
    in_four = lax.rem(me, 4)

    def at_sub(offset):
        return lax.rem(me + offset + subs, subs)

    def in_group(x):
        return me - in_eight + jnp.bitwise_xor(in_eight, x)

    barrier = pltpu.get_barrier_semaphore()
    greeted = 0
    for x in range(1, 8):
        pl.semaphore_signal(barrier, inc=1, device_id=(in_group(x), mo), device_id_type=MESH)
        greeted += 1
    for q in (-2, -1, 1, 2):
        pl.semaphore_signal(barrier, inc=1, device_id=(at_sub(q), mo), device_id_type=MESH)
        greeted += 1
    for x in range(1, peers_mode):
        other = lax.rem(mo + x, peers_mode)
        pl.semaphore_signal(barrier, inc=1, device_id=(me, other), device_id_type=MESH)
        greeted += 1

    rows[...] = jnp.full(rows.shape, -1, jnp.int32)
    own1 = a1.at[:, pl.ds(pl.multiple_of(odd * 128, 128), 128)]
    own2 = a2.at[pl.ds(pl.multiple_of(in_four * 64, 64), 64), :]
    own3 = a3.at[pl.ds(pl.multiple_of(in_eight * 32, 32), 32), :]
    loads = [
        pltpu.make_async_copy(rows_h, rows.at[pl.ds(0, CLS), :], in_sem.at[0]),
        pltpu.make_async_copy(s3_h, own3, in_sem.at[1]),
        pltpu.make_async_copy(s2_h, own2, in_sem.at[2]),
        pltpu.make_async_copy(s1_h, own1, in_sem.at[3]),
        pltpu.make_async_copy(lc_h, lc, in_sem.at[4]),
        pltpu.make_async_copy(comp_h, comp, in_sem.at[5]),
        pltpu.make_async_copy(mw_h, mw, in_sem.at[6]),
        pltpu.make_async_copy(ops_h, ops, in_sem.at[7]),
    ]
    for load in loads[:4]:
        load.start()
    def leaf_load(l):
        return pltpu.make_async_copy(lm_h.at[l], w.at[l, pl.ds(0, KL), :], leaf_sem.at[l])

    def cm_load(l):
        return pltpu.make_async_copy(cm_h.at[l], w.at[l, pl.ds(KL, 3 * B), :], cm_sem.at[l])

    loads[4].start()
    for l in range(NLEAF):
        leaf_load(l).start()
        cm_load(l).start()
    for load in loads[5:]:
        load.start()

    pl.semaphore_wait(barrier, greeted)

    chip, chip_of_two = in_eight // 2, in_four // 2
    sibling = in_group(1)

    def core_one(x):
        return me - in_eight + 2 * jnp.bitwise_xor(chip, x) + 1

    def sep_copy(src, dst, sent, landed, target):
        return pltpu.make_async_remote_copy(
            src_ref=src,
            dst_ref=dst,
            send_sem=sep_send.at[sent],
            recv_sem=sep_recv.at[landed],
            device_id=(target, mo),
            device_id_type=MESH,
        )

    sep_copies = [
        sep_copy(s2_h, own2, 0, 6 + odd, core_one(1)),
        sep_copy(s3_h, own3, 1, odd, core_one(1)),
        sep_copy(s3_h, own3, 2, 2 + odd, core_one(2)),
        sep_copy(s3_h, own3, 3, 4 + odd, core_one(3)),
        sep_copy(s1_h, own1, 4, 10, sibling),
        sep_copy(s2_h, own2, 5, 9, sibling),
        sep_copy(s3_h, own3, 6, 8, sibling),
    ]
    for copy in sep_copies:
        copy.start()
    other_two = a2.at[pl.ds(pl.multiple_of(128 * (1 - chip_of_two), 128), 128), :]
    pass_on = [sep_copy(other_two, other_two, 7, 11, sibling)]
    for x in (1, 2, 3):
        rows_of = pl.ds(pl.multiple_of(64 * jnp.bitwise_xor(chip, x), 64), 64)
        pass_on.append(sep_copy(a3.at[rows_of, :], a3.at[rows_of, :], 7 + x, 11 + x, sibling))

    table[...] = (lax.broadcasted_iota(jnp.int32, (R, 128), 0) - 256).astype(F32).astype(BF16)
    earlier = (
        lax.broadcasted_iota(jnp.int32, (CW, CW), 0) < lax.broadcasted_iota(jnp.int32, (CW, CW), 1)
    )
    earlier = jnp.where(earlier, 1.0, 0.0).astype(BF16)
    loads[0].wait()
    ids = rows[...]
    off = jnp.bitwise_and(jnp.right_shift(ids, 12) - me + 2, subs - 1)
    off = jnp.where(ids < 0, -1, off)
    local = jnp.bitwise_and(ids, DOFS - 1)
    masks = jnp.concatenate([(off == o).astype(F32) for o in range(NOFF + 1)], axis=0)
    ranks = mm(masks.astype(BF16), earlier)
    totals = jnp.sum(masks, axis=1, keepdims=True)
    line = lax.broadcasted_iota(jnp.int32, (8, 1), 0)
    wanted = []
    slot = jnp.full((8, CW), -1, jnp.int32)
    for o in range(NOFF):
        count = totals[8 * o : 8 * o + 8]
        base = jnp.where(line >= 1, count[0:1], 0.0) + jnp.where(line >= 2, count[1:2], 0.0)
        rank = ranks[8 * o : 8 * o + 8] + base
        wanted.append(jnp.where(off == o, rank - SLOT // 2, 999.0))
        slot = jnp.where(off == o, rank.astype(jnp.int32) + SLOT * o, slot)
    slot_row, slot_col = jnp.right_shift(slot, 7), jnp.bitwise_and(slot, 127)
    high, low = jnp.right_shift(local, 6), jnp.bitwise_and(local, 63)
    sixteen = lax.broadcasted_iota(jnp.int32, (16, CW), 0)
    left, right = [], []
    for c in range(CLS):
        here = slot_row[c : c + 1] == sixteen
        both = [jnp.where(here, part[c : c + 1], 0) for part in (high, low)]
        left.append(jnp.concatenate(both, axis=0).astype(F32).astype(BF16))
        right.append(one_hot(table[256:384], slot_col[c : c + 1].astype(F32)))
    found = lax.dot_general(
        jnp.concatenate(left, axis=1),
        jnp.concatenate(right, axis=1),
        (((1,), (1,)), ((), ())),
        preferred_element_type=F32,
    )
    found = (found[0:16] * 64.0 + found[16:32]).astype(jnp.int32)
    for r in range(3 * NOFF):
        lists[r] = found[r : r + 1]

    def list_copy(o, target):
        return pltpu.make_async_remote_copy(
            src_ref=lists.at[pl.ds(3 * o, 3)],
            dst_ref=want.at[pl.ds(3 * o, 3)],
            send_sem=list_send.at[o],
            recv_sem=list_recv.at[o],
            device_id=(target, mo),
            device_id_type=MESH,
        )

    far = (0, 4, 1, 3)
    list_copies = [list_copy(o, at_sub(o - 2)) for o in far]
    for copy in list_copies:
        copy.start()

    for o in range(NOFF):
        for c in range(CLS):
            hit = one_hot(table[256 - SLOT // 2 : 256 + SLOT // 2], wanted[o][c : c + 1])
            pick[o, :, c * CW : (c + 1) * CW] = hit

    loads[3].wait()
    loads[4].wait()
    sep_copies[4].wait_recv()
    for l in range(NLEAF):
        leaf_load(l).wait()
        cm_load(l).wait()
        x = jnp.concatenate([lc[l], a1[...]], axis=1)
        acc[l] = mm(x, w[l, 0 : KL + B, :])

    for load in loads[1:3]:
        load.wait()
    for copy in sep_copies[5:]:
        copy.wait_recv()

    @pl.when(odd == 1)
    def _():
        for k in range(2):
            sep_copy(s2_h, own2, 0, 6 + k, sibling).wait_recv()
        pass_on[0].start()
        for x in (1, 2, 3):
            for k in range(2):
                sep_copy(s3_h, own3, x, 2 * (x - 1) + k, sibling).wait_recv()
            pass_on[x].start()

    @pl.when(odd == 0)
    def _():
        for copy in pass_on:
            copy.wait_recv()

    x23[:, 0:B] = jnp.transpose(a2[...])
    x23[:, B : 2 * B] = jnp.transpose(a3[...])
    for l in range(NLEAF):
        both = acc[l] + mm(x23[...], w[l, KL + B : KL + 3 * B, :])
        disp[:, l * R : (l + 1) * R] = both.astype(BF16)

    def hot_rows(wish, into):
        for l in range(NLEAF):
            here = jnp.right_shift(wish, 9) == l
            v = jnp.where(here, jnp.bitwise_and(wish, R - 1) - 256, 999).astype(F32)
            into[l * R : (l + 1) * R, :] = one_hot(table[...], v)

    third = 3 - 2 * odd
    fourth = 4 - third

    def data_copy(r, target):
        return pltpu.make_async_remote_copy(
            src_ref=gath.at[r],
            dst_ref=got.at[r],
            send_sem=data_send.at[r],
            recv_sem=data_recv.at[r],
            device_id=(target, mo),
            device_id_type=MESH,
        )

    for copy in list_copies:
        copy.wait_recv()

    @pl.loop(0, 6)
    def _(t):
        late = t // 3
        part = lax.rem(t, 3)
        o1 = late * third
        o2 = 4 - o1
        r1, r2 = 3 * o1 + part, 3 * o2 + part
        hot_rows(jnp.concatenate([want[r1], want[r2]], axis=1), hot)
        both = mm(disp[...], hot[...]).astype(BF16)
        gath[r1] = both[:, 0:128]
        data_copy(r1, at_sub(2 - o1)).start()
        gath[r2] = both[:, 128:256]
        data_copy(r2, at_sub(2 - o2)).start()

    hot_rows(jnp.concatenate([lists[6], lists[7], lists[8]], axis=1), own_hot)
    own = mm(disp[...], own_hot[...]).astype(BF16)

    def arrived(o):
        for part in range(3):
            data_copy(3 * o + part, me).wait_recv()
        return [got[3 * o + part] for part in range(3)]

    x = jnp.concatenate([own] + arrived(third), axis=1)
    rhs = jnp.concatenate([pick[2], pick[third]], axis=0)
    cols32[...] = mm(x, rhs)
    x = jnp.concatenate(arrived(0) + arrived(4), axis=1)
    cols32[...] += mm(x, jnp.concatenate([pick[0], pick[4]], axis=0))
    for load in loads[5:]:
        load.wait()
    eye = lax.broadcasted_iota(jnp.int32, (MODES, MODES), 0) == lax.broadcasted_iota(
        jnp.int32, (MODES, MODES), 1
    )
    weight = jnp.sum(jnp.where(eye, mw[...], 0.0), axis=1, keepdims=True)
    x = jnp.concatenate(arrived(fourth), axis=1)
    cols[...] = (cols32[...] + mm(x, pick[fourth])).astype(BF16)
    energies = []
    for c in range(CLS):
        s = mm(cols[:, c * CW : (c + 1) * CW], ops[c])
        stress[c] = s
        e = jnp.sum(s * s * weight, axis=0, keepdims=True) * comp[c : c + 1]
        e = e[:, 0:128] + e[:, 128:256] + e[:, 256:384]
        energies.append((e + pltpu.roll(e, 64, 1)) * (0.5 / M))
    half = lax.broadcasted_iota(jnp.int32, (1, 128), 1) < 64
    terms[mo] = jnp.concatenate([jnp.where(half, energies[0], energies[1]), energies[2]], axis=1)
    en_copies = []
    for x in range(1, peers_mode):
        other = lax.rem(mo + x, peers_mode)
        copy = pltpu.make_async_remote_copy(
            src_ref=terms.at[mo],
            dst_ref=terms.at[mo],
            send_sem=en_send.at[x],
            recv_sem=en_recv.at[x],
            device_id=(me, other),
            device_id_type=MESH,
        )
        copy.start()
        en_copies.append(copy)

    for copy in sep_copies:
        copy.wait_send()

    @pl.when(odd == 1)
    def _():
        for copy in pass_on:
            copy.wait_send()

    for copy in list_copies:
        copy.wait_send()
    for o in far:
        for part in range(3):
            data_copy(3 * o + part, me).wait_send()
    for copy in en_copies:
        copy.wait_recv()
    total = terms[0]
    for x in range(1, peers_mode):
        total = total + terms[x]
    share = CLS * 64 // peers_mode
    total = pltpu.roll(total, lax.rem(256 - share * mo, 256), 1)
    energy[...] = total[:, 0:share]
    for copy in en_copies:
        copy.wait_send()


def hand_out(stress_v, energy_v, stress_h, energy_h, sem):
    copies = [pltpu.make_async_copy(energy_v, energy_h, sem.at[CLS])]
    for c in range(CLS):
        copies.append(pltpu.make_async_copy(stress_v.at[c], stress_h.at[c], sem.at[c]))
    for copy in copies:
        copy.start()
    for copy in copies:
        copy.wait()


def shards(lc, lm, cm, s1, s2, s3, rows, ops, comp, mw):
    subs = lax.axis_size("sub")
    peers_mode = lax.axis_size("mode")
    share = CLS * 64 // peers_mode
    anywhere = pl.BlockSpec(memory_space=pl.ANY)
    vmem = pl.BlockSpec(memory_space=pltpu.VMEM)
    dma = pltpu.SemaphoreType.DMA
    values = (
        lc,
        lm,
        cm.reshape(NLEAF, 3 * B, R),
        s1,
        s2.T,
        s3.T,
        rows,
        ops,
        comp,
        mw.reshape(1, MODES),
    )
    stress, energy = pl.pallas_call(
        functools.partial(kernel, subs, peers_mode),
        out_shape=(
            pltpu.VMEM((CLS, MODES, SR), F32),
            pltpu.VMEM((1, share), F32),
        ),
        in_specs=[anywhere] * 10,
        out_specs=(vmem, vmem),
        scratch_shapes=[
            pltpu.VMEM((NLEAF, MODES, KL), BF16),
            pltpu.VMEM((NLEAF, KL + 3 * B, R), BF16),
            pltpu.VMEM((MODES, B), BF16),
            pltpu.VMEM((B, MODES), BF16),
            pltpu.VMEM((B, MODES), BF16),
            pltpu.VMEM((MODES, 2 * B), BF16),
            pltpu.VMEM((8, CW), jnp.int32),
            pltpu.VMEM((CLS, CW, SR), BF16),
            pltpu.VMEM((CLS, SR), F32),
            pltpu.VMEM((1, MODES), F32),
            pltpu.VMEM((NLEAF, MODES, R), F32),
            pltpu.VMEM((MODES, DOFS), BF16),
            pltpu.VMEM((R, 128), BF16),
            pltpu.VMEM((NOFF, SLOT, CLS * CW), BF16),
            pltpu.VMEM((3 * NOFF, 1, 128), jnp.int32),
            pltpu.VMEM((3 * NOFF, 1, 128), jnp.int32),
            pltpu.VMEM((DOFS, 256), BF16),
            pltpu.VMEM((DOFS, SLOT), BF16),
            pltpu.VMEM((3 * NOFF, MODES, 128), BF16),
            pltpu.VMEM((3 * NOFF, MODES, 128), BF16),
            pltpu.VMEM((MODES, CLS * CW), F32),
            pltpu.VMEM((MODES, CLS * CW), BF16),
            pltpu.VMEM((peers_mode, 1, 256), F32),
            dma((8,)),
            dma((NLEAF,)),
            dma((NLEAF,)),
            dma((11,)),
            dma((15,)),
            dma((NOFF,)),
            dma((NOFF,)),
            dma((3 * NOFF,)),
            dma((3 * NOFF,)),
            dma((4,)),
            dma((4,)),
        ],
        compiler_params=pltpu.CompilerParams(
            collective_id=0, has_side_effects=True, vmem_limit_bytes=44 * 2**20
        ),
        name="back_transform",
    )(*[pltpu.with_memory_space_constraint(value, pltpu.HBM) for value in values])
    stress, energy = pl.pallas_call(
        hand_out,
        out_shape=(
            jax.ShapeDtypeStruct((CLS, MODES, SR), F32),
            jax.ShapeDtypeStruct((1, share), F32),
        ),
        in_specs=[anywhere] * 2,
        out_specs=(anywhere, anywhere),
        scratch_shapes=[dma((CLS + 1,))],
        compiler_params=pltpu.CompilerParams(vmem_limit_bytes=16 * 2**20),
        name="hand_out",
    )(stress, energy)
    return stress, energy.reshape(share)


def solution(mesh):
    return jax.shard_map(
        shards,
        mesh=mesh,
        in_specs=(
            P("sub", "mode", None),
            P("sub", None, None),
            P("sub", None, None, None),
            P("mode", "sub"),
            P("mode", "sub"),
            P("mode", "sub"),
            P("sub", None),
            P("sub", None, None),
            P("sub", None),
            P("mode"),
        ),
        out_specs=(P("sub", "mode", None), P(("sub", "mode"))),
        check_vma=False,
    )
```

```python
import functools

import jax
import jax.numpy as jnp
from jax import lax
from jax.experimental import pallas as pl
from jax.experimental.pallas import tpu as pltpu
from jax.sharding import PartitionSpec as P

M = 768
F32, BF16 = jnp.float32, jnp.bfloat16
MODES, NLEAF, KL, R, B = 192, 8, 128, 512, 256
DOFS = NLEAF * R
CLS, CW, SR = 3, 512, 384
SLOT, NOFF = 384, 5
MESH = pl.DeviceIdType.MESH


def mm(a, b):
    return jnp.dot(a, b, preferred_element_type=F32)


def one_hot(table, values):
    n, w = table.shape[0], values.shape[1]
    wide = jnp.broadcast_to(values, (16, w)).astype(BF16).reshape(1, 16, w)
    rows = jnp.concatenate([table.reshape(n // 16, 16, 128)] * (w // 128), axis=2)
    hit = rows == jnp.broadcast_to(wide, (n // 16, 16, w))
    return jnp.where(hit, jnp.ones((), BF16), jnp.zeros((), BF16)).reshape(n, w)


def kernel(
    subs,
    peers_mode,
    lc_h,
    lm_h,
    cm_h,
    s1_h,
    s2_h,
    s3_h,
    rows_h,
    ops_h,
    comp_h,
    mw_h,
    stress,
    energy,
    lc,
    w,
    a1,
    a2,
    a3,
    x23,
    rows,
    ops,
    comp,
    mw,
    acc,
    disp,
    table,
    pick,
    lists,
    want,
    hot,
    own_hot,
    gath,
    got,
    cols32,
    cols,
    terms,
    in_sem,
    leaf_sem,
    cm_sem,
    sep_send,
    sep_recv,
    list_send,
    list_recv,
    data_send,
    data_recv,
    en_send,
    en_recv,
):
    me = lax.axis_index("sub")
    mo = lax.axis_index("mode")
    odd = lax.rem(me, 2)
    in_eight = lax.rem(me, 8)
    in_four = lax.rem(me, 4)

    def at_sub(offset):
        return lax.rem(me + offset + subs, subs)

    def in_group(x):
        return me - in_eight + jnp.bitwise_xor(in_eight, x)

    barrier = pltpu.get_barrier_semaphore()
    greeted = 0
    for x in range(1, 8):
        pl.semaphore_signal(barrier, inc=1, device_id=(in_group(x), mo), device_id_type=MESH)
        greeted += 1
    for q in (-2, -1, 1, 2):
        pl.semaphore_signal(barrier, inc=1, device_id=(at_sub(q), mo), device_id_type=MESH)
        greeted += 1
    for x in range(1, peers_mode):
        other = lax.rem(mo + x, peers_mode)
        pl.semaphore_signal(barrier, inc=1, device_id=(me, other), device_id_type=MESH)
        greeted += 1

    rows[...] = jnp.full(rows.shape, -1, jnp.int32)
    own1 = a1.at[:, pl.ds(pl.multiple_of(odd * 128, 128), 128)]
    own2 = a2.at[pl.ds(pl.multiple_of(in_four * 64, 64), 64), :]
    own3 = a3.at[pl.ds(pl.multiple_of(in_eight * 32, 32), 32), :]
    loads = [
        pltpu.make_async_copy(rows_h, rows.at[pl.ds(0, CLS), :], in_sem.at[0]),
        pltpu.make_async_copy(s3_h, own3, in_sem.at[1]),
        pltpu.make_async_copy(s2_h, own2, in_sem.at[2]),
        pltpu.make_async_copy(s1_h, own1, in_sem.at[3]),
        pltpu.make_async_copy(lc_h, lc, in_sem.at[4]),
        pltpu.make_async_copy(comp_h, comp, in_sem.at[5]),
        pltpu.make_async_copy(mw_h, mw, in_sem.at[6]),
        pltpu.make_async_copy(ops_h, ops, in_sem.at[7]),
    ]
    for load in loads[:4]:
        load.start()
    def leaf_load(l):
        return pltpu.make_async_copy(lm_h.at[l], w.at[l, pl.ds(0, KL), :], leaf_sem.at[l])

    def cm_load(l):
        return pltpu.make_async_copy(cm_h.at[l], w.at[l, pl.ds(KL, 3 * B), :], cm_sem.at[l])

    loads[4].start()
    for l in range(NLEAF):
        leaf_load(l).start()
        cm_load(l).start()
    for load in loads[5:]:
        load.start()

    table[...] = (lax.broadcasted_iota(jnp.int32, (R, 128), 0) - 256).astype(F32).astype(BF16)
    earlier = (
        lax.broadcasted_iota(jnp.int32, (CW, CW), 0) < lax.broadcasted_iota(jnp.int32, (CW, CW), 1)
    )
    earlier = jnp.where(earlier, 1.0, 0.0).astype(BF16)
    loads[0].wait()
    ids = rows[...]
    off = jnp.bitwise_and(jnp.right_shift(ids, 12) - me + 2, subs - 1)
    off = jnp.where(ids < 0, -1, off)
    local = jnp.bitwise_and(ids, DOFS - 1)
    masks = jnp.concatenate([(off == o).astype(F32) for o in range(NOFF + 1)], axis=0)
    ranks = mm(masks.astype(BF16), earlier)
    totals = jnp.sum(masks, axis=1, keepdims=True)
    line = lax.broadcasted_iota(jnp.int32, (8, 1), 0)
    wanted = []
    slot = jnp.full((8, CW), -1, jnp.int32)
    for o in range(NOFF):
        count = totals[8 * o : 8 * o + 8]
        base = jnp.where(line >= 1, count[0:1], 0.0) + jnp.where(line >= 2, count[1:2], 0.0)
        rank = ranks[8 * o : 8 * o + 8] + base
        wanted.append(jnp.where(off == o, rank - SLOT // 2, 999.0))
        slot = jnp.where(off == o, rank.astype(jnp.int32) + SLOT * o, slot)
    slot_row, slot_col = jnp.right_shift(slot, 7), jnp.bitwise_and(slot, 127)
    high, low = jnp.right_shift(local, 6), jnp.bitwise_and(local, 63)
    sixteen = lax.broadcasted_iota(jnp.int32, (16, CW), 0)
    left, right = [], []
    for c in range(CLS):
        here = slot_row[c : c + 1] == sixteen
        both = [jnp.where(here, part[c : c + 1], 0) for part in (high, low)]
        left.append(jnp.concatenate(both, axis=0).astype(F32).astype(BF16))
        right.append(one_hot(table[256:384], slot_col[c : c + 1].astype(F32)))
    found = lax.dot_general(
        jnp.concatenate(left, axis=1),
        jnp.concatenate(right, axis=1),
        (((1,), (1,)), ((), ())),
        preferred_element_type=F32,
    )
    found = (found[0:16] * 64.0 + found[16:32]).astype(jnp.int32)
    for r in range(3 * NOFF):
        lists[r] = found[r : r + 1]

    pl.semaphore_wait(barrier, greeted)

    chip, chip_of_two = in_eight // 2, in_four // 2
    sibling = in_group(1)

    def core_one(x):
        return me - in_eight + 2 * jnp.bitwise_xor(chip, x) + 1

    def sep_copy(src, dst, sent, landed, target):
        return pltpu.make_async_remote_copy(
            src_ref=src,
            dst_ref=dst,
            send_sem=sep_send.at[sent],
            recv_sem=sep_recv.at[landed],
            device_id=(target, mo),
            device_id_type=MESH,
        )

    sep_copies = [
        sep_copy(s2_h, own2, 0, 6 + odd, core_one(1)),
        sep_copy(s3_h, own3, 1, odd, core_one(1)),
        sep_copy(s3_h, own3, 2, 2 + odd, core_one(2)),
        sep_copy(s3_h, own3, 3, 4 + odd, core_one(3)),
        sep_copy(s1_h, own1, 4, 10, sibling),
        sep_copy(s2_h, own2, 5, 9, sibling),
        sep_copy(s3_h, own3, 6, 8, sibling),
    ]
    for n in (4, 1, 2, 3, 0, 5, 6):
        sep_copies[n].start()
    other_two = a2.at[pl.ds(pl.multiple_of(128 * (1 - chip_of_two), 128), 128), :]
    pass_on = [sep_copy(other_two, other_two, 7, 11, sibling)]
    for x in (1, 2, 3):
        rows_of = pl.ds(pl.multiple_of(64 * jnp.bitwise_xor(chip, x), 64), 64)
        pass_on.append(sep_copy(a3.at[rows_of, :], a3.at[rows_of, :], 7 + x, 11 + x, sibling))

    def list_copy(o, target):
        return pltpu.make_async_remote_copy(
            src_ref=lists.at[pl.ds(3 * o, 3)],
            dst_ref=want.at[pl.ds(3 * o, 3)],
            send_sem=list_send.at[o],
            recv_sem=list_recv.at[o],
            device_id=(target, mo),
            device_id_type=MESH,
        )

    far = (0, 4, 1, 3)
    list_copies = [list_copy(o, at_sub(o - 2)) for o in far]
    for copy in list_copies:
        copy.start()

    for o in range(NOFF):
        for c in range(CLS):
            hit = one_hot(table[256 - SLOT // 2 : 256 + SLOT // 2], wanted[o][c : c + 1])
            pick[o, :, c * CW : (c + 1) * CW] = hit

    loads[3].wait()
    loads[4].wait()
    sep_copies[4].wait_recv()
    for l in range(NLEAF):
        leaf_load(l).wait()
        cm_load(l).wait()
        x = jnp.concatenate([lc[l], a1[...]], axis=1)
        acc[l] = mm(x, w[l, 0 : KL + B, :])

    for load in loads[1:3]:
        load.wait()
    for copy in sep_copies[5:]:
        copy.wait_recv()

    @pl.when(odd == 1)
    def _():
        for k in range(2):
            sep_copy(s2_h, own2, 0, 6 + k, sibling).wait_recv()
        pass_on[0].start()
        for x in (1, 2, 3):
            for k in range(2):
                sep_copy(s3_h, own3, x, 2 * (x - 1) + k, sibling).wait_recv()
            pass_on[x].start()

    @pl.when(odd == 0)
    def _():
        for copy in pass_on:
            copy.wait_recv()

    x23[:, 0:B] = jnp.transpose(a2[...])
    x23[:, B : 2 * B] = jnp.transpose(a3[...])
    for l in range(NLEAF):
        both = acc[l] + mm(x23[...], w[l, KL + B : KL + 3 * B, :])
        disp[:, l * R : (l + 1) * R] = both.astype(BF16)

    def hot_rows(wish, into):
        for l in range(NLEAF):
            here = jnp.right_shift(wish, 9) == l
            v = jnp.where(here, jnp.bitwise_and(wish, R - 1) - 256, 999).astype(F32)
            into[l * R : (l + 1) * R, :] = one_hot(table[...], v)

    third = 3 - 2 * odd
    fourth = 4 - third

    def data_copy(r, target):
        return pltpu.make_async_remote_copy(
            src_ref=gath.at[r],
            dst_ref=got.at[r],
            send_sem=data_send.at[r],
            recv_sem=data_recv.at[r],
            device_id=(target, mo),
            device_id_type=MESH,
        )

    for copy in list_copies:
        copy.wait_recv()

    @pl.loop(0, 6)
    def _(t):
        late = t // 3
        part = lax.rem(t, 3)
        o1 = late * third
        o2 = 4 - o1
        r1, r2 = 3 * o1 + part, 3 * o2 + part
        hot_rows(jnp.concatenate([want[r1], want[r2]], axis=1), hot)
        both = mm(disp[...], hot[...]).astype(BF16)
        gath[r1] = both[:, 0:128]
        data_copy(r1, at_sub(2 - o1)).start()
        gath[r2] = both[:, 128:256]
        data_copy(r2, at_sub(2 - o2)).start()

    hot_rows(jnp.concatenate([lists[6], lists[7], lists[8]], axis=1), own_hot)
    own = mm(disp[...], own_hot[...]).astype(BF16)

    def arrived(o):
        for part in range(3):
            data_copy(3 * o + part, me).wait_recv()
        return [got[3 * o + part] for part in range(3)]

    x = jnp.concatenate([own] + arrived(third), axis=1)
    rhs = jnp.concatenate([pick[2], pick[third]], axis=0)
    cols32[...] = mm(x, rhs)
    x = jnp.concatenate(arrived(0) + arrived(4), axis=1)
    cols32[...] += mm(x, jnp.concatenate([pick[0], pick[4]], axis=0))
    for load in loads[5:]:
        load.wait()
    eye = lax.broadcasted_iota(jnp.int32, (MODES, MODES), 0) == lax.broadcasted_iota(
        jnp.int32, (MODES, MODES), 1
    )
    weight = jnp.sum(jnp.where(eye, mw[...], 0.0), axis=1, keepdims=True)
    x = jnp.concatenate(arrived(fourth), axis=1)
    cols[...] = (cols32[...] + mm(x, pick[fourth])).astype(BF16)
    energies = []
    for c in range(CLS):
        s = mm(cols[:, c * CW : (c + 1) * CW], ops[c])
        stress[c] = s
        e = jnp.sum(s * s * weight, axis=0, keepdims=True) * comp[c : c + 1]
        e = e[:, 0:128] + e[:, 128:256] + e[:, 256:384]
        energies.append((e + pltpu.roll(e, 64, 1)) * (0.5 / M))
    half = lax.broadcasted_iota(jnp.int32, (1, 128), 1) < 64
    terms[mo] = jnp.concatenate([jnp.where(half, energies[0], energies[1]), energies[2]], axis=1)
    en_copies = []
    for x in (2, 1, 3):
        other = lax.rem(mo + x, peers_mode)
        copy = pltpu.make_async_remote_copy(
            src_ref=terms.at[mo],
            dst_ref=terms.at[mo],
            send_sem=en_send.at[x],
            recv_sem=en_recv.at[x],
            device_id=(me, other),
            device_id_type=MESH,
        )
        copy.start()
        en_copies.append(copy)

    for copy in sep_copies:
        copy.wait_send()

    @pl.when(odd == 1)
    def _():
        for copy in pass_on:
            copy.wait_send()

    for copy in list_copies:
        copy.wait_send()
    for o in far:
        for part in range(3):
            data_copy(3 * o + part, me).wait_send()
    for copy in en_copies:
        copy.wait_recv()
    total = terms[0]
    for x in range(1, peers_mode):
        total = total + terms[x]
    share = CLS * 64 // peers_mode
    total = pltpu.roll(total, lax.rem(256 - share * mo, 256), 1)
    energy[...] = total[:, 0:share]
    for copy in en_copies:
        copy.wait_send()


def hand_out(stress_v, energy_v, stress_h, energy_h, sem):
    copies = [pltpu.make_async_copy(energy_v, energy_h, sem.at[CLS])]
    for c in range(CLS):
        copies.append(pltpu.make_async_copy(stress_v.at[c], stress_h.at[c], sem.at[c]))
    for copy in copies:
        copy.start()
    for copy in copies:
        copy.wait()


def shards(lc, lm, cm, s1, s2, s3, rows, ops, comp, mw):
    subs = lax.axis_size("sub")
    peers_mode = lax.axis_size("mode")
    share = CLS * 64 // peers_mode
    anywhere = pl.BlockSpec(memory_space=pl.ANY)
    vmem = pl.BlockSpec(memory_space=pltpu.VMEM)
    dma = pltpu.SemaphoreType.DMA
    values = (
        lc,
        lm,
        cm.reshape(NLEAF, 3 * B, R),
        s1,
        s2.T,
        s3.T,
        rows,
        ops,
        comp,
        mw.reshape(1, MODES),
    )
    stress, energy = pl.pallas_call(
        functools.partial(kernel, subs, peers_mode),
        out_shape=(
            pltpu.VMEM((CLS, MODES, SR), F32),
            pltpu.VMEM((1, share), F32),
        ),
        in_specs=[anywhere] * 10,
        out_specs=(vmem, vmem),
        scratch_shapes=[
            pltpu.VMEM((NLEAF, MODES, KL), BF16),
            pltpu.VMEM((NLEAF, KL + 3 * B, R), BF16),
            pltpu.VMEM((MODES, B), BF16),
            pltpu.VMEM((B, MODES), BF16),
            pltpu.VMEM((B, MODES), BF16),
            pltpu.VMEM((MODES, 2 * B), BF16),
            pltpu.VMEM((8, CW), jnp.int32),
            pltpu.VMEM((CLS, CW, SR), BF16),
            pltpu.VMEM((CLS, SR), F32),
            pltpu.VMEM((1, MODES), F32),
            pltpu.VMEM((NLEAF, MODES, R), F32),
            pltpu.VMEM((MODES, DOFS), BF16),
            pltpu.VMEM((R, 128), BF16),
            pltpu.VMEM((NOFF, SLOT, CLS * CW), BF16),
            pltpu.VMEM((3 * NOFF, 1, 128), jnp.int32),
            pltpu.VMEM((3 * NOFF, 1, 128), jnp.int32),
            pltpu.VMEM((DOFS, 256), BF16),
            pltpu.VMEM((DOFS, SLOT), BF16),
            pltpu.VMEM((3 * NOFF, MODES, 128), BF16),
            pltpu.VMEM((3 * NOFF, MODES, 128), BF16),
            pltpu.VMEM((MODES, CLS * CW), F32),
            pltpu.VMEM((MODES, CLS * CW), BF16),
            pltpu.VMEM((peers_mode, 1, 256), F32),
            dma((8,)),
            dma((NLEAF,)),
            dma((NLEAF,)),
            dma((11,)),
            dma((15,)),
            dma((NOFF,)),
            dma((NOFF,)),
            dma((3 * NOFF,)),
            dma((3 * NOFF,)),
            dma((4,)),
            dma((4,)),
        ],
        compiler_params=pltpu.CompilerParams(
            collective_id=0, has_side_effects=True, vmem_limit_bytes=44 * 2**20
        ),
        name="back_transform",
    )(*[pltpu.with_memory_space_constraint(value, pltpu.HBM) for value in values])
    stress, energy = pl.pallas_call(
        hand_out,
        out_shape=(
            jax.ShapeDtypeStruct((CLS, MODES, SR), F32),
            jax.ShapeDtypeStruct((1, share), F32),
        ),
        in_specs=[anywhere] * 2,
        out_specs=(anywhere, anywhere),
        scratch_shapes=[dma((CLS + 1,))],
        compiler_params=pltpu.CompilerParams(vmem_limit_bytes=16 * 2**20),
        name="hand_out",
    )(stress, energy)
    return stress, energy.reshape(share)


def solution(mesh):
    return jax.shard_map(
        shards,
        mesh=mesh,
        in_specs=(
            P("sub", "mode", None),
            P("sub", None, None),
            P("sub", None, None, None),
            P("mode", "sub"),
            P("mode", "sub"),
            P("mode", "sub"),
            P("sub", None),
            P("sub", None, None),
            P("sub", None),
            P("mode"),
        ),
        out_specs=(P("sub", "mode", None), P(("sub", "mode"))),
        check_vma=False,
    )
```
